32 devices in a mesh: groups: 2 (over y), rows: 4 (over z), proj: 4 (over x, core).
Axes of the slice: x: 2, y: 2, z: 4, core: 2. Of those that a mesh axis runs over, the one named last changes fastest.
Arguments:
- targets: bfloat16 [256, 8192], P('proj', 'rows'), may hold values from -6 to 6
- precond: bfloat16 [16384, 8192], P(('groups', 'rows'), 'proj'), parts along dimension 0, may hold values from -0.0625 to 0.0625
- train_grads: bfloat16 [12288, 8192], P(('groups', 'rows'), 'proj'), parts along dimension 0, may hold values from -0.0625 to 0.0625
Outputs:
- scores: float32 [256, 12288], P('proj', ('groups', 'rows')), parts along dimension 1
The draws below stay inside these ranges and needn't reach their ends.
There are 2 independent parts, one for each index of `groups`. The reference program is written for one: setup_inputs(seed, part) draws one part's arguments, and reference() takes and returns one part's arrays. A program takes and returns all parts, laid end to end along the dimension named above; an argument that names none is the same for every part. Nothing has to cross between parts.
All inputs are finite; a program needn't handle non-finite values.
Results may differ from the reference program's by a relative error of at most 0.015.
Values may be sent and summed in bfloat16 or wider, within the bound.
No kernel may reach another device: no remote copies, remote signals or barrier semaphores. Data moves between devices by JAX's collectives and lax.ppermute only.
A program may use at most 64 MiB of HBM per device.

```python
import jax
import jax.numpy as jnp

K = 8192
M = 256
NTRAIN = 6144
N_PROJ = 4


def block_levels(own_key, shape, shards, least, top_value):
    factor_of, own = 1.0, jax.random.fold_in(own_key, 6)
    for axis_at, blocks in shards:
        steps = jnp.exp(jax.random.uniform(jax.random.fold_in(own, axis_at), (blocks,), jnp.float32, least / len(shards), top_value / len(shards)))
        factor_of = factor_of * jnp.repeat(steps, shape[axis_at] // blocks).reshape([-1 if axis == axis_at else 1 for axis in range(len(shape))])
    return factor_of


def gaussian(stream_key, shape, scale, bound, cuts=(), dtype=jnp.bfloat16):
    factor_of = block_levels(stream_key, shape, cuts, -0.22, 0.18) if cuts else 1.0
    drawn = jax.random.normal(stream_key, shape, jnp.float32) * scale * factor_of
    return jnp.minimum(jnp.maximum(drawn, -bound), bound).astype(dtype)


def setup_inputs(seed: int = 0, part: int = 0) -> dict:
    key_list = jax.random.split(jax.random.key(seed), 4)
    own_keys = jax.random.split(jax.random.fold_in(key_list[3], part), 4)
    return {
        "targets": gaussian(key_list[0], (M, K), 1.0, 6.0, ((0, 4), (1, 4))),
        "precond": gaussian(own_keys[1], (K, K), K ** -0.5, 0.0625, ((0, 4), (1, 4))),
        "train_grads": gaussian(own_keys[2], (NTRAIN, K), K ** -0.5, 0.0625, ((0, 4), (1, 4))),
    }


def reference(targets, precond, train_grads):
    conditioned = jnp.dot(targets, precond, preferred_element_type=jnp.float32).astype(jnp.bfloat16)
    width = K // N_PROJ
    total = jnp.zeros((M, NTRAIN), jnp.float32)
    for block in range(N_PROJ):
        left = conditioned[:, block * width:(block + 1) * width]
        right = train_grads[:, block * width:(block + 1) * width]
        part = jnp.dot(left, right.T, preferred_element_type=jnp.float32).astype(jnp.bfloat16)
        total = total + part.astype(jnp.float32)
    return total
```

```python
import jax
import jax.numpy as jnp
from jax import lax
from jax.experimental import pallas as pl
from jax.experimental.pallas import tpu as pltpu
from jax.sharding import PartitionSpec as P

VMEM = pl.BlockSpec(memory_space=pltpu.VMEM)
SMEM = pl.BlockSpec(memory_space=pltpu.SMEM)
LIMIT = pltpu.CompilerParams(vmem_limit_bytes=32 << 20)
BF16, F32 = jnp.bfloat16, jnp.float32


def apply_precond(rows, precond):
    m, n = rows.shape[0], precond.shape[1]
    step = min(n, 512)

    def kernel(rows_ref, precond_ref, out_ref):
        for at in range(0, n, step):
            out_ref[:, at : at + step] = jnp.dot(
                rows_ref[...], precond_ref[:, at : at + step], preferred_element_type=F32
            ).astype(BF16)

    return pl.pallas_call(
        kernel,
        out_shape=jax.ShapeDtypeStruct((m, n), BF16),
        in_specs=[VMEM, VMEM],
        out_specs=VMEM,
        compiler_params=LIMIT,
        cost_estimate=pl.CostEstimate(
            flops=2 * m * precond.size, bytes_accessed=precond.size * 2, transcendentals=0
        ),
    )(rows, precond)


def score(outer, kept, given, train):
    m, n = kept.shape[0], train.shape[0]
    step = n // 3

    def kernel(outer_ref, kept_ref, given_ref, train_ref, out_ref):
        left = jnp.where(outer_ref[0] == 1, given_ref[...], kept_ref[...])
        for at in range(0, n, step):
            out_ref[:, at : at + step] = lax.dot_general(
                left, train_ref[at : at + step, :], (((1,), (1,)), ((), ())), preferred_element_type=F32
            ).astype(BF16)

    return pl.pallas_call(
        kernel,
        out_shape=jax.ShapeDtypeStruct((m, n), BF16),
        in_specs=[SMEM, VMEM, VMEM, VMEM],
        out_specs=VMEM,
        compiler_params=LIMIT,
        cost_estimate=pl.CostEstimate(
            flops=2 * m * train.size, bytes_accessed=train.size * 2, transcendentals=0
        ),
    )(outer, kept, given, train)


def add(a, b):
    def kernel(a_ref, b_ref, out_ref):
        out_ref[...] = (a_ref[...].astype(F32) + b_ref[...].astype(F32)).astype(BF16)

    return pl.pallas_call(
        kernel,
        out_shape=jax.ShapeDtypeStruct(a.shape, BF16),
        in_specs=[VMEM, VMEM],
        out_specs=VMEM,
        compiler_params=LIMIT,
    )(a, b)


def make_body(n_rows, n_proj):
    half = n_rows // 2
    inward = [[(h, h + 1), (n_rows - 1 - h, n_rows - 2 - h)] for h in range(half - 1)]
    middle = [(half - 1, half), (half, half - 1)]
    outward = [[(b, a) for a, b in pairs] for pairs in reversed(inward)]

    def across(x, d):
        return lax.ppermute(x, "proj", [(i, i ^ d) for i in range(n_proj)])

    def body(targets, precond, train):
        z = lax.axis_index("rows")
        m = targets.shape[0]
        rows = {0: targets, 1: across(targets, 1)}
        for d in range(2, n_proj, 2):
            rows[d] = across(targets, d)
            rows[d + 1] = across(rows[d], 1)
        owners = [0, 1] + [d ^ 1 for d in range(2, n_proj)]
        cond = {d: apply_precond(rows[d], precond) for d in owners}
        chunks = [(0, 0, m // 2)] + [(d, 0, m) for d in owners[1:]] + [(0, m // 2, m)]
        parts = {}
        for d, lo, hi in chunks:
            total = cond[d][lo:hi]
            for pairs in inward:
                total = add(total, lax.ppermute(total, "rows", pairs))
            total = add(total, lax.ppermute(total, "rows", middle))
            for hop, pairs in enumerate(outward):
                given = lax.ppermute(total, "rows", pairs)
                edge = half - 2 - hop
                outer = ((z == edge) | (z == n_rows - 1 - edge)).astype(jnp.int32)
                if hop < len(outward) - 1:
                    total = jnp.where(outer == 1, given, total)
            parts[d, lo] = score(outer[None], total, given, train)
        got = jnp.concatenate([parts[0, 0], parts[0, m // 2]]).astype(F32)
        for d in owners[1:]:
            got = got + across(parts[d, 0], d).astype(F32)
        return got

    return body


def solution(mesh):
    return jax.shard_map(
        make_body(mesh.shape["rows"], mesh.shape["proj"]),
        mesh=mesh,
        in_specs=(P("proj", "rows"), P(("groups", "rows"), "proj"), P(("groups", "rows"), "proj")),
        out_specs=P("proj", ("groups", "rows")),
        check_vma=False,
    )
```

```python
import jax
import jax.numpy as jnp
from jax import lax
from jax.experimental import pallas as pl
from jax.experimental.pallas import tpu as pltpu
from jax.sharding import PartitionSpec as P

VMEM = pl.BlockSpec(memory_space=pltpu.VMEM)
LIMIT = pltpu.CompilerParams(vmem_limit_bytes=12 << 20)
BF16, F32 = jnp.bfloat16, jnp.float32


def dot(a, b):
    return jnp.dot(a, b, preferred_element_type=F32)


def dot_t(a, b):
    return lax.dot_general(a, b, (((1,), (1,)), ((), ())), preferred_element_type=F32)


class Order:
    def __init__(self):
        self.last = ()

    def __call__(self, kernel, shapes, *args, cost=0):
        n_args, n_extra = len(args), len(self.last)

        def ordered(*refs):
            kernel(*refs[:n_args], *refs[n_args + n_extra :])

        outs = pl.pallas_call(
            ordered,
            out_shape=tuple(pltpu.VMEM(shape, dtype) for shape, dtype in shapes),
            in_specs=[VMEM] * (n_args + n_extra),
            out_specs=(VMEM,) * len(shapes),
            compiler_params=LIMIT,
            cost_estimate=pl.CostEstimate(flops=0, bytes_accessed=cost, transcendentals=0),
        )(*args, *self.last)
        self.last = (outs[0],)
        return outs


def make_body(n_rows, n_proj):
    half = n_rows // 2
    hops = half - 1
    n_chunks = n_proj

    def both_ways(pairs):
        partner = {i: j for a, b in pairs for i, j in ((a, b), (b, a))}
        swaps = []
        for z in range(n_rows):
            for p in range(n_proj):
                to = (partner[z], p) if z in partner else (z, p ^ 1)
                swaps.append((z * n_proj + p, to[0] * n_proj + to[1]))
        return swaps

    hop_swaps = [both_ways([(h, h + 1), (n_rows - 1 - h, n_rows - 2 - h)]) for h in range(hops)]
    middle_swaps = both_ways([(half - 1, half)])

    def along(x, swaps):
        return lax.ppermute(x, ("rows", "proj"), swaps)

    def across(x, d):
        return lax.ppermute(x, "proj", [(i, i ^ d) for i in range(n_proj)])

    def at(h):
        z = lax.axis_index("rows")
        return (z == h) | (z == n_rows - 1 - h)

    def body(targets, precond, train):
        call = Order()
        m = targets.shape[0]
        n, t = precond.shape[1], train.shape[0]

        def elementwise(function, *args):
            def kernel(*refs):
                *in_refs, out_ref = refs
                out_ref[...] = function(*[r[...] for r in in_refs])

            return call(kernel, [(args[0].shape, BF16)], *args)[0]

        def plus(a, b):
            return (a.astype(F32) + b.astype(F32)).astype(BF16)

        def condition(*rows):
            step = min(n, 512)

            def kernel(*refs):
                row_refs, precond_ref, out_refs = refs[: len(rows)], refs[len(rows)], refs[len(rows) + 1 :]
                left = jnp.concatenate([r[...] for r in row_refs])
                for lo in range(0, n, step):
                    cols = slice(lo, lo + step)
                    value = dot(left, precond_ref[:, cols]).astype(BF16)
                    for i, out_ref in enumerate(out_refs):
                        out_ref[:, cols] = value[i * m : (i + 1) * m]

            return call(kernel, [((m, n), BF16)] * len(rows), *rows, precond)

        def scores(kept, given, dtype):
            step = t // 3

            def kernel(kept_ref, given_ref, train_ref, out_ref):
                left = jnp.where(at(0), given_ref[...], kept_ref[...])
                for lo in range(0, t, step):
                    cols = slice(lo, lo + step)
                    out_ref[:, cols] = dot_t(left, train_ref[cols, :]).astype(dtype)

            return call(kernel, [((m, t), dtype)], kept, given, train)[0]

        (staged,) = call(lambda x_ref, out_ref: out_ref.__setitem__(..., x_ref[...]), [(targets.shape, BF16)], targets, cost=40 << 20)
        rows = {0: staged, 1: across(staged, 1), 2: across(staged, 2)}
        owners = [*range(1, n_proj), 0]
        here, total, parts = {}, {}, {}

        def begin(c):
            here[c] = condition(rows[owners[c]])[0]

        here[0], here[n_chunks - 1] = condition(rows[1], rows[0])
        again = elementwise(lambda x: x, staged)
        for d in range(3, n_proj):
            rows[d] = across(again, d)

        moving = {}

        def valid(c):
            return 0 <= c < n_chunks

        def start_hop(h, step):
            inward, outward = step - h, step - 2 * hops + h
            if valid(inward) and valid(outward):
                value = elementwise(lambda a, b: jnp.where(at(h), a, b), here[inward], total[outward])
            elif valid(inward):
                value = here[inward]
            elif valid(outward):
                value = total[outward]
            else:
                return
            moving[h, step] = along(value, hop_swaps[h])

        def end_hop_inward(h, step):
            c = step - h
            if valid(c):
                here[c] = elementwise(
                    lambda a, b: jnp.where(at(h + 1), plus(a, b), a), here[c], moving[h, step]
                )

        def end_hop_outward(h, step):
            c = step - 2 * hops + h
            if valid(c) and h > 0:
                total[c] = elementwise(lambda a, b: jnp.where(at(h), b, a), total[c], moving[h, step])

        def finish(c):
            d = owners[c]
            value = scores(total[c], moving[0, c + 2 * hops], BF16 if d else F32)
            parts[d] = across(value, d) if d else value

        start_hop(0, 0)
        begun = 1
        for step in range(1, n_chunks + 2 * hops + 2):
            if begun < n_chunks - 1:
                begin(begun)
                begun += 1
            if step < 2 * hops:
                start_hop(0, step)
            for h in reversed(range(hops)):
                end_hop_inward(h, step - 1)
            if valid(step - hops):
                moving["middle", step] = along(here[step - hops], middle_swaps)
            if valid(step - 1 - hops):
                c = step - 1 - hops
                total[c] = elementwise(plus, here[c], moving["middle", step - 1])
            for h in range(hops):
                end_hop_outward(h, step - 1)
            for h in reversed(range(hops)):
                if h > 0 or step >= 2 * hops:
                    start_hop(h, step)
            if valid(step - 1 - 2 * hops):
                finish(step - 1 - 2 * hops)

        def close(own_ref, *refs):
            *got_refs, out_ref = refs
            value = own_ref[...]
            for ref in got_refs:
                value = value + ref[...].astype(F32)
            out_ref[...] = value

        return call(close, [((m, t), F32)], *[parts[d] for d in range(n_proj)])[0]

    return body


def solution(mesh):
    return jax.shard_map(
        make_body(mesh.shape["rows"], mesh.shape["proj"]),
        mesh=mesh,
        in_specs=(P("proj", "rows"), P(("groups", "rows"), "proj"), P(("groups", "rows"), "proj")),
        out_specs=P("proj", ("groups", "rows")),
        check_vma=False,
    )
```

```python
import jax
import jax.numpy as jnp
from jax import lax
from jax.experimental import pallas as pl
from jax.experimental.pallas import tpu as pltpu
from jax.sharding import PartitionSpec as P

VMEM = pl.BlockSpec(memory_space=pltpu.VMEM)
ANY = pl.BlockSpec(memory_space=pl.ANY)
BF16, F32 = jnp.bfloat16, jnp.float32
SPLIT = 1
LAG = 1


def dot(a, b):
    return jnp.dot(a, b, preferred_element_type=F32)


def dot_t(a, b):
    return lax.dot_general(a, b, (((1,), (1,)), ((), ())), preferred_element_type=F32)


class Order:
    def __init__(self):
        self.last = ()

    def __call__(self, kernel, shapes, *args, in_place=(), scratch=(), limit=12 << 20):
        n_args, n_extra = len(args), len(self.last)

        def ordered(*refs):
            kernel(*refs[:n_args], *refs[n_args + n_extra :])

        outs = pl.pallas_call(
            ordered,
            out_shape=tuple(pltpu.VMEM(shape, dtype) for shape, dtype in shapes),
            in_specs=[ANY if i in in_place else VMEM for i in range(n_args)] + [VMEM] * n_extra,
            out_specs=(VMEM,) * len(shapes),
            scratch_shapes=scratch,
            compiler_params=pltpu.CompilerParams(vmem_limit_bytes=limit),
            cost_estimate=pl.CostEstimate(flops=0, bytes_accessed=0, transcendentals=0),
        )(*args, *self.last)
        self.last = (outs[0],)
        return outs


def make_body(n_rows, n_proj):
    half = n_rows // 2
    hops = half - 1

    def both_ways(pairs):
        partner = {i: j for a, b in pairs for i, j in ((a, b), (b, a))}
        swaps = []
        for z in range(n_rows):
            for p in range(n_proj):
                to = (partner[z], p) if z in partner else (z, p ^ 1)
                swaps.append((z * n_proj + p, to[0] * n_proj + to[1]))
        return swaps

    hop_swaps = [both_ways([(h, h + 1), (n_rows - 1 - h, n_rows - 2 - h)]) for h in range(hops)]
    middle_swaps = both_ways([(half - 1, half)])

    def along(x, swaps):
        return lax.ppermute(x, ("rows", "proj"), swaps)

    def across(x, d):
        return lax.ppermute(x, "proj", [(i, i ^ d) for i in range(n_proj)])

    def at(h):
        z = lax.axis_index("rows")
        return (z == h) | (z == n_rows - 1 - h)

    def body(targets, precond, train):
        call = Order()
        m, k = targets.shape
        n, t = precond.shape[1], train.shape[0]
        size = m // SPLIT

        def elementwise(function, *args):
            small = min(x.shape[0] for x in args)
            longest = max(range(len(args)), key=lambda i: args[i].shape[0])
            large = args[longest].shape[0]

            def kernel(*refs):
                *in_refs, out_ref = refs
                out_ref[:small] = function(*[r[:small] for r in in_refs])
                if large > small:
                    out_ref[small:] = in_refs[longest][small:]

            return call(kernel, [((large, *args[0].shape[1:]), BF16)], *args)[0]

        def update(function, kept, got):
            def kernel(kept_ref, got_ref, out_ref):
                out_ref[...] = function(kept_ref[...], got_ref[: kept.shape[0]])

            return call(kernel, [(kept.shape, BF16)], kept, got)[0]

        def plus(a, b):
            return (a.astype(F32) + b.astype(F32)).astype(BF16)

        def first_condition(left):
            blocks = 8 if k % (8 * 256) == 0 else 1
            step, width = k // blocks, min(n, 512)

            def kernel(left_ref, precond_hbm, *refs):
                *out_refs, precond_ref, sum_ref, sems = refs
                copies = []
                for i in range(blocks):
                    part = pl.ds(i * step, step)
                    copies.append(pltpu.make_async_copy(precond_hbm.at[part], precond_ref.at[part], sems.at[i]))
                    copies[i].start()
                for i in range(blocks):
                    copies[i].wait()
                    part = slice(i * step, (i + 1) * step)
                    for lo in range(0, n, width):
                        cols = slice(lo, lo + width)
                        value = dot(left_ref[:, part], precond_ref[part, cols])
                        if i > 0:
                            value = value + sum_ref[:, cols]
                        if i < blocks - 1:
                            sum_ref[:, cols] = value
                        else:
                            for j, out_ref in enumerate(out_refs):
                                out_ref[:, cols] = value[j * size : (j + 1) * size].astype(BF16)

            *out, kept = call(
                kernel,
                [((size, n), BF16)] * SPLIT + [(precond.shape, BF16)],
                left,
                pltpu.with_memory_space_constraint(precond, pltpu.HBM),
                in_place=(1,),
                scratch=(pltpu.VMEM((m, n), F32), pltpu.SemaphoreType.DMA((blocks,))),
            )
            return out, kept

        def condition(*lefts):
            step = min(n, 512)
            count = len(lefts) * SPLIT

            def kernel(*refs):
                left_refs, precond_ref, out_refs = refs[: len(lefts)], refs[len(lefts)], refs[len(lefts) + 1 :]
                left = jnp.concatenate([r[...] for r in left_refs])
                for lo in range(0, n, step):
                    cols = slice(lo, lo + step)
                    value = dot(left, precond_ref[:, cols]).astype(BF16)
                    for j, out_ref in enumerate(out_refs):
                        out_ref[:, cols] = value[j * size : (j + 1) * size]

            return call(kernel, [((size, n), BF16)] * count, *lefts, weights)

        def scores(groups, dtype):
            step = t // 3

            def kernel(*refs):
                total_refs, train_ref, out_refs = refs[: -1 - len(groups)], refs[-1 - len(groups)], refs[-len(groups) :]
                left = jnp.concatenate([r[...] for r in total_refs])
                for lo in range(0, t, step):
                    cols = slice(lo, lo + step)
                    value = dot_t(left, train_ref[cols, :]).astype(dtype)
                    for j, out_ref in enumerate(out_refs):
                        out_ref[:, cols] = value[j * m : (j + 1) * m]

            return call(kernel, [((m, t), dtype)] * len(groups), *sum(groups, []), train)

        owners = [1, *[d ^ 1 for d in range(2, n_proj)], 0]
        n_chunks = n_proj * SPLIT
        rows = {0: targets}
        here, total, parts, moving = {}, {}, {}, {}

        def same(x):
            return elementwise(lambda v: v, x)

        def fetch(i, value):
            rows[owners[i]] = across(value, owners[i])

        def begin(*group):
            new = condition(*[rows[owners[i]] for i in group])
            here.update(zip([c for i in group for c in range(i * SPLIT, (i + 1) * SPLIT)], new, strict=True))

        def valid(c):
            return 0 <= c < n_chunks

        def outward(h, step):
            return step - 2 * hops + h - LAG

        def start_hop(h, step):
            c, back = step - h, outward(h, step)
            if valid(c) and valid(back):
                value = elementwise(lambda a, b: jnp.where(at(h), a, b), here[c], total[back])
            elif valid(c):
                value = same(here[c]) if step > 0 else here[c]
            elif valid(back):
                value = same(total[back])
            else:
                return
            moving[h, step] = along(value, hop_swaps[h])

        def end_hop(h, step):
            c, back = step - h, outward(h, step)
            if valid(c):
                here[c] = update(lambda a, b: jnp.where(at(h + 1), plus(a, b), a), here[c], moving[h, step])
            if valid(back):
                total[back] = update(lambda a, b: jnp.where(at(h), b, a), total[back], moving[h, step])

        def gather(i):
            def kernel(*refs):
                *in_refs, out_ref = refs
                value = in_refs[0][...].astype(F32)
                for ref in in_refs[1:]:
                    value = value + ref[...].astype(F32)
                out_ref[...] = value

            terms = ([parts["sum"]] if "sum" in parts else []) + [parts[i]]
            parts["sum"] = call(kernel, [((m, t), F32)], *terms)[0]

        def finish(*group):
            values = scores([[total[c] for c in range(i * SPLIT, (i + 1) * SPLIT)] for i in group], F32 if owners[group[0]] == 0 else BF16)
            for i, value in zip(group, values):
                parts[i] = across(value, owners[i]) if owners[i] else value

        rows[1] = across(targets, 1)
        fetch(1, targets)
        first, weights = first_condition(rows[1])
        here.update(enumerate(first))
        start_hop(0, 0)
        if n_proj > 3:
            fetch(2, same(targets))
        begin(1)
        start_hop(0, 1)
        finished = 0
        for step in range(1, n_chunks + 2 * hops + LAG + 1):
            for h in reversed(range(hops)):
                end_hop(h, step - 1)
            c = step - hops
            if valid(c):
                moving["middle", step] = along(here[c], middle_swaps)
            for h in range(1, hops):
                start_hop(h, step)
            i = step // SPLIT + 1
            if step % SPLIT == 0 and 1 < i < n_proj - 1:
                if i + 1 < n_proj - 1:
                    fetch(i + 1, same(targets))
                begin(*([i] if i < n_proj - 2 else [i, i + 1]))
            c = step - 1 - 2 * hops - LAG
            if valid(c) and c % SPLIT == SPLIT - 1:
                i = c // SPLIT
                if i > 0:
                    finish(*([i] if i > 1 else [0, 1]))
                if 1 < i < n_proj - 1:
                    gather(i - 2)
                    gather(i - 1) if i == n_proj - 2 else None
            c = step - 1 - hops
            if valid(c):
                total[c] = update(plus, here[c], moving["middle", step - 1])
            start_hop(0, step + 1)

        gather(n_proj - 2)
        gather(n_proj - 1)
        return parts["sum"]

    return body


def solution(mesh):
    return jax.shard_map(
        make_body(mesh.shape["rows"], mesh.shape["proj"]),
        mesh=mesh,
        in_specs=(P("proj", "rows"), P(("groups", "rows"), "proj"), P(("groups", "rows"), "proj")),
        out_specs=P("proj", ("groups", "rows")),
        check_vma=False,
    )
```

```python
import jax
import jax.numpy as jnp
from jax import lax
from jax.experimental import pallas as pl
from jax.experimental.pallas import tpu as pltpu
from jax.sharding import PartitionSpec as P

VMEM = pl.BlockSpec(memory_space=pltpu.VMEM)
ANY = pl.BlockSpec(memory_space=pl.ANY)
BF16, F32 = jnp.bfloat16, jnp.float32
WORK = 2 * 10**9
LAG = 1


def dot(a, b):
    return jnp.dot(a, b, preferred_element_type=F32)


def dot_t(a, b):
    return lax.dot_general(a, b, (((1,), (1,)), ((), ())), preferred_element_type=F32)


class Order:
    def __init__(self):
        self.last = ()

    def __call__(self, name, kernel, shapes, *args, in_place=(), scratch=(), work=0):
        n_args, n_extra = len(args), len(self.last)

        def ordered(*refs):
            kernel(*refs[:n_args], *refs[n_args + n_extra :])

        outs = pl.pallas_call(
            ordered,
            name=name,
            out_shape=tuple(pltpu.VMEM(shape, dtype) for shape, dtype in shapes),
            in_specs=[ANY if i in in_place else VMEM for i in range(n_args)] + [VMEM] * n_extra,
            out_specs=(VMEM,) * len(shapes),
            scratch_shapes=scratch,
            compiler_params=pltpu.CompilerParams(vmem_limit_bytes=12 << 20),
            cost_estimate=pl.CostEstimate(flops=work, bytes_accessed=0, transcendentals=0),
        )(*args, *self.last)
        self.last = (outs[0],)
        return outs


def make_body(n_rows, n_proj):
    half = n_rows // 2
    hops = half - 1

    def both_ways(pairs):
        partner = {i: j for a, b in pairs for i, j in ((a, b), (b, a))}
        swaps = []
        for z in range(n_rows):
            for p in range(n_proj):
                to = (partner[z], p) if z in partner else (z, p ^ 1)
                swaps.append((z * n_proj + p, to[0] * n_proj + to[1]))
        return swaps

    hop_swaps = [both_ways([(h, h + 1), (n_rows - 1 - h, n_rows - 2 - h)]) for h in range(hops)]
    middle_swaps = both_ways([(half - 1, half)])

    def along(x, swaps):
        return lax.ppermute(x, ("rows", "proj"), swaps)

    def across(x, d):
        return lax.ppermute(x, "proj", [(i, i ^ d) for i in range(n_proj)])

    def at(h):
        z = lax.axis_index("rows")
        return (z == h) | (z == n_rows - 1 - h)

    def body(targets, precond, train):
        call = Order()
        m, k = targets.shape
        n, t = precond.shape[1], train.shape[0]

        half_n = n // 2
        halves = (slice(0, half_n), slice(half_n, n))

        def elementwise(name, function, *args):
            small = min(x.shape[0] for x in args)
            longest = max(range(len(args)), key=lambda i: args[i].shape[0])
            large = args[longest].shape[0]

            def kernel(*refs):
                *in_refs, out_ref = refs
                out_ref[:small] = function(*[r[:small] for r in in_refs])
                if large > small:
                    out_ref[small:] = in_refs[longest][small:]

            return call(name, kernel, [((large, args[0].shape[1]), BF16)], *args, work=WORK)[0]

        def update(name, function, kept, got):
            def kernel(kept_ref, got_ref, out_ref):
                out_ref[...] = function(kept_ref[...], got_ref[: kept.shape[0]])

            return call(name, kernel, [(kept.shape, BF16)], kept, got, work=WORK)[0]

        def plus(a, b):
            return (a.astype(F32) + b.astype(F32)).astype(BF16)

        def read_condition(left, side):
            blocks = 4 if k % (4 * 256) == 0 else 1
            step, width = k // blocks, min(half_n, 512)

            def kernel(left_ref, precond_hbm, out_ref, precond_ref, sum_ref, sems):
                copies = []
                for i in range(blocks):
                    part = pl.ds(i * step, step)
                    source = precond_hbm.at[part, pl.ds(side * half_n, half_n)]
                    copies.append(pltpu.make_async_copy(source, precond_ref.at[part], sems.at[i]))
                    copies[i].start()
                for i in range(blocks):
                    copies[i].wait()
                    part = slice(i * step, (i + 1) * step)
                    for lo in range(0, half_n, width):
                        cols = slice(lo, lo + width)
                        value = dot(left_ref[:, part], precond_ref[part, cols])
                        if i > 0:
                            value = value + sum_ref[:, cols]
                        if i < blocks - 1:
                            sum_ref[:, cols] = value
                        else:
                            out_ref[:, cols] = value.astype(BF16)

            return call(
                f"read_condition_{side}",
                kernel,
                [((m, half_n), BF16), ((k, half_n), BF16)],
                left,
                pltpu.with_memory_space_constraint(precond, pltpu.HBM),
                in_place=(1,),
                scratch=(pltpu.VMEM((m, half_n), F32), pltpu.SemaphoreType.DMA((blocks,))),
            )

        def condition(name, left, ranges):
            step = min(half_n, 512)

            def kernel(left_ref, low_ref, high_ref, *out_refs):
                for side, ref in zip(halves, (low_ref, high_ref)):
                    for lo in range(0, half_n, step):
                        value = dot(left_ref[...], ref[:, lo : lo + step]).astype(BF16)
                        cols = slice(side.start + lo, side.start + lo + step)
                        for (top, end), out_ref in zip(ranges, out_refs):
                            out_ref[:, cols] = value[top:end]

            return call(name, kernel, [((end - top, n), BF16) for top, end in ranges], left, *weights, work=WORK)

        def transposed(x):
            step = min(512, x.shape[1])
            wide = t // 3 if t % 384 == 0 else t

            def kernel(x_ref, out_ref):
                for top in range(0, t, wide):
                    for lo in range(0, x.shape[1], step):
                        out_ref[lo : lo + step, top : top + wide] = x_ref[top : top + wide, lo : lo + step].T

            return call("transposed_train", kernel, [((x.shape[1], t), BF16)], x, work=WORK)[0]

        def scores(name, chunk, left, cols):
            def kernel(left_ref, train_ref, out_ref):
                out_ref[...] = dot(left_ref[...], train_ref[:, cols]).astype(BF16)

            return call(name, kernel, [((left.shape[0], cols.stop - cols.start), BF16)], left, trained[0], work=WORK if chunk < last - 1 else 0)[0]

        def last_scores(side, kept, given, *before):
            step = t // 3

            def kernel(kept_ref, given_ref, train_ref, *refs):
                *before_refs, out_ref = refs
                left = jnp.where(at(0), given_ref[...], kept_ref[...])
                for lo in range(0, t, step):
                    cols = slice(lo, lo + step)
                    value = dot(left, train_ref[halves[side], cols])
                    for ref in before_refs:
                        value = value + ref[:, cols]
                    out_ref[:, cols] = value

            return call(f"last_scores_{side}", kernel, [((m, t), F32)], kept, given, trained[0], *before)[0]

        owners = [1, *[d ^ 1 for d in range(2, n_proj)], 0]
        ranges = {d: [(0, m)] for d in owners}
        chunks = [(d, *r) for d in owners for r in ranges[d]]
        n_chunks = len(chunks)
        last = n_chunks - 1
        rows = {0: targets}
        here, total, parts, moving = {}, {}, {}, {}

        def same(name, x):
            return elementwise(name, lambda v: v, x)

        def fetch(i, value):
            rows[owners[i]] = across(value, owners[i])

        def begin(i):
            d = owners[i]
            first = chunks.index((d, *ranges[d][0]))
            here.update(enumerate(condition(f"condition_{i}", rows[d], ranges[d]), first))

        def valid(c):
            return 0 <= c < n_chunks

        back_at = 2 * hops + LAG + (hops > 1)

        def outward(h, step):
            return step - back_at if h == 0 else step - 2 * hops + h - LAG

        def start_hop(h, step):
            c, back = step - h, outward(h, step)
            if h == 0 and c == 0:
                moving[h, step] = [along(x, hop_swaps[h]) for x in here[c]]
                return
            if h == 0 and back == last:
                if hops > 1:

                    def kernel(x_ref, *out_refs):
                        for side, out_ref in zip(halves, out_refs):
                            out_ref[...] = x_ref[:, side]

                    total[back] = call("halves", kernel, [((m, half_n), BF16)] * 2, total[back])
                moving[h, step] = [along(x, hop_swaps[h]) for x in total[back]]
                return
            if valid(c) and valid(back):
                value = elementwise(f"merge_{step}", lambda a, b: jnp.where(at(h), a, b), here[c], total[back])
            elif valid(c):
                value = same(f"pass_{step}", here[c])
            elif valid(back):
                value = same(f"back_{step}", total[back])
            else:
                return
            moving[h, step] = along(value, hop_swaps[h])

        def end_hop(h, step):
            c, back = step - h, outward(h, step)

            def absorb(a, b):
                return jnp.where(at(h + 1), plus(a, b), a)

            if h == 0 and c == 0:
                low = update("absorb_0a", absorb, here[c][0], moving[h, step][0])

                def kernel(low_ref, a_ref, b_ref, out_ref):
                    out_ref[:, halves[0]] = low_ref[...]
                    out_ref[:, halves[1]] = absorb(a_ref[...], b_ref[...])

                here[c] = call("absorb_0b", kernel, [((m, n), BF16)], low, here[c][1], moving[h, step][1], work=WORK)[0]
            elif valid(c):
                here[c] = update(f"absorb_{step}", absorb, here[c], moving[h, step])
            if valid(back) and not (h == 0 and back == last):
                total[back] = update(f"adopt_{back}", lambda a, b: jnp.where(at(h), b, a), total[back], moving[h, step])

        def end_middle(c, step):
            if c == last and hops == 1:

                def kernel(a_ref, b_ref, *out_refs):
                    for side, out_ref in zip(halves, out_refs):
                        out_ref[...] = plus(a_ref[:, side], b_ref[:, side])

                total[c] = call("total_last", kernel, [((m, half_n), BF16)] * 2, here[c], moving["middle", step])
            else:
                total[c] = update(f"total_{c}", plus, here[c], moving["middle", step])

        def gather(c):
            for i, (cols, got) in enumerate(zip(pieces(c), parts[c])):
                first = c == 0 and i == 0

                def kernel(*refs):
                    *in_refs, out_ref = refs
                    if first:
                        out_ref[...] = jnp.zeros_like(out_ref)
                    else:
                        out_ref[...] = in_refs[0][...]
                    out_ref[:, cols] += in_refs[-1][...].astype(F32)

                before = [] if first else [parts["sum"]]
                parts["sum"] = call(f"gather_{c}_{i}", kernel, [((m, t), F32)], *before, got, work=WORK if c == last - 1 and i == 0 else 0)[0]

        def pieces(c):
            if c == last - 1 and t % 256 == 0:
                return [slice(0, t // 2), slice(t // 2, t)]
            return [slice(0, t)]

        def finish(c):
            parts[c] = []
            for i, cols in enumerate(pieces(c)):
                parts[c].append(across(scores(f"scores_{c}_{i}", c, total[c], cols), chunks[c][0]))

        for i in range(min(3, n_proj - 1)):
            fetch(i, targets)
        weights = []
        here[0] = []
        for side in (0, 1):
            out, half_weights = read_condition(rows[1], side)
            here[0].append(out)
            weights.append(half_weights)
        start_hop(0, 0)
        begin(1)
        start_hop(0, 1)
        trained = []
        for step in range(1, n_chunks + back_at):
            for h in reversed(range(hops)):
                end_hop(h, step - 1)
            c = step - hops
            if valid(c):
                moving["middle", step] = along(here[c], middle_swaps)
            for h in range(1, hops):
                start_hop(h, step)
            if step == 1:
                begin(n_proj - 1)
            if step + 1 < n_proj - 1:
                if step + 2 < n_proj - 1:
                    fetch(step + 2, same(f"own_rows_{step}", targets))
                begin(step + 1)
            c = step - 1 - back_at
            if valid(c):
                finish(c)
            if step == 2:
                trained.append(transposed(train))
            c = step - 1 - hops
            if valid(c):
                end_middle(c, step - 1)
            start_hop(0, step + 1)
        for c in range(last - 1):
            gather(c)
        value = None
        for side in (0, 1):
            before = [] if value is None else [value]
            value = last_scores(side, total[last][side], moving[0, last + back_at][side], *before)
        gather(last - 1)

        def close(sum_ref, value_ref, out_ref):
            out_ref[...] = sum_ref[...] + value_ref[...]

        return call("close", close, [((m, t), F32)], parts["sum"], value)[0]

    return body


def solution(mesh):
    return jax.shard_map(
        make_body(mesh.shape["rows"], mesh.shape["proj"]),
        mesh=mesh,
        in_specs=(P("proj", "rows"), P(("groups", "rows"), "proj"), P(("groups", "rows"), "proj")),
        out_specs=P("proj", ("groups", "rows")),
        check_vma=False,
    )
```

```python
import jax
import jax.numpy as jnp
from jax import lax
from jax.experimental import pallas as pl
from jax.experimental.pallas import tpu as pltpu
from jax.sharding import PartitionSpec as P

VMEM = pl.BlockSpec(memory_space=pltpu.VMEM)
ANY = pl.BlockSpec(memory_space=pl.ANY)
BF16, F32 = jnp.bfloat16, jnp.float32
WORK = 2 * 10**9
LAG = 1


def dot(a, b):
    return jnp.dot(a, b, preferred_element_type=F32)


def dot_t(a, b):
    return lax.dot_general(a, b, (((1,), (1,)), ((), ())), preferred_element_type=F32)


class Order:
    def __init__(self):
        self.last = ()

    def __call__(self, name, kernel, shapes, *args, in_place=(), scratch=(), work=0):
        n_args, n_extra = len(args), len(self.last)

        def ordered(*refs):
            kernel(*refs[:n_args], *refs[n_args + n_extra :])

        outs = pl.pallas_call(
            ordered,
            name=name,
            out_shape=tuple(pltpu.VMEM(shape, dtype) for shape, dtype in shapes),
            in_specs=[ANY if i in in_place else VMEM for i in range(n_args)] + [VMEM] * n_extra,
            out_specs=(VMEM,) * len(shapes),
            scratch_shapes=scratch,
            compiler_params=pltpu.CompilerParams(vmem_limit_bytes=12 << 20),
            cost_estimate=pl.CostEstimate(flops=work, bytes_accessed=0, transcendentals=0),
        )(*args, *self.last)
        self.last = (outs[0],)
        return outs


def make_body(n_rows, n_proj):
    half = n_rows // 2
    hops = half - 1

    def both_ways(pairs):
        partner = {i: j for a, b in pairs for i, j in ((a, b), (b, a))}
        swaps = []
        for z in range(n_rows):
            for p in range(n_proj):
                to = (partner[z], p) if z in partner else (z, p ^ 1)
                swaps.append((z * n_proj + p, to[0] * n_proj + to[1]))
        return swaps

    hop_swaps = [both_ways([(h, h + 1), (n_rows - 1 - h, n_rows - 2 - h)]) for h in range(hops)]
    middle_swaps = both_ways([(half - 1, half)])

    def along(x, swaps):
        return lax.ppermute(x, ("rows", "proj"), swaps)

    def across(x, d):
        return lax.ppermute(x, "proj", [(i, i ^ d) for i in range(n_proj)])

    def at(h):
        z = lax.axis_index("rows")
        return (z == h) | (z == n_rows - 1 - h)

    def body(targets, precond, train):
        call = Order()
        m, k = targets.shape
        n, t = precond.shape[1], train.shape[0]

        half_n = n // 2
        halves = (slice(0, half_n), slice(half_n, n))

        def elementwise(name, function, *args):
            small = min(x.shape[0] for x in args)
            longest = max(range(len(args)), key=lambda i: args[i].shape[0])
            large = args[longest].shape[0]

            def kernel(*refs):
                *in_refs, out_ref = refs
                out_ref[:small] = function(*[r[:small] for r in in_refs])
                if large > small:
                    out_ref[small:] = in_refs[longest][small:]

            return call(name, kernel, [((large, args[0].shape[1]), BF16)], *args, work=WORK)[0]

        def update(name, function, kept, got):
            def kernel(kept_ref, got_ref, out_ref):
                out_ref[...] = function(kept_ref[...], got_ref[: kept.shape[0]])

            return call(name, kernel, [(kept.shape, BF16)], kept, got, work=WORK)[0]

        def plus(a, b):
            return (a.astype(F32) + b.astype(F32)).astype(BF16)

        def read_condition(left, side):
            blocks = 4 if k % (4 * 256) == 0 else 1
            step, width = k // blocks, min(half_n, 512)

            def kernel(left_ref, precond_hbm, out_ref, precond_ref, sum_ref, sems):
                copies = []
                for i in range(blocks):
                    part = pl.ds(i * step, step)
                    source = precond_hbm.at[part, pl.ds(side * half_n, half_n)]
                    copies.append(pltpu.make_async_copy(source, precond_ref.at[part], sems.at[i]))
                    copies[i].start()
                for i in range(blocks):
                    copies[i].wait()
                    part = slice(i * step, (i + 1) * step)
                    for lo in range(0, half_n, width):
                        cols = slice(lo, lo + width)
                        value = dot(left_ref[:, part], precond_ref[part, cols])
                        if i > 0:
                            value = value + sum_ref[:, cols]
                        if i < blocks - 1:
                            sum_ref[:, cols] = value
                        else:
                            out_ref[:, cols] = value.astype(BF16)

            return call(
                f"read_condition_{side}",
                kernel,
                [((m, half_n), BF16), ((k, half_n), BF16)],
                left,
                pltpu.with_memory_space_constraint(precond, pltpu.HBM),
                in_place=(1,),
                scratch=(pltpu.VMEM((m, half_n), F32), pltpu.SemaphoreType.DMA((blocks,))),
            )

        def condition(name, left, ranges):
            step = min(half_n, 512)

            def kernel(left_ref, low_ref, high_ref, *out_refs):
                for side, ref in zip(halves, (low_ref, high_ref)):
                    for lo in range(0, half_n, step):
                        value = dot(left_ref[...], ref[:, lo : lo + step]).astype(BF16)
                        cols = slice(side.start + lo, side.start + lo + step)
                        for (top, end), out_ref in zip(ranges, out_refs):
                            out_ref[:, cols] = value[top:end]

            return call(name, kernel, [((end - top, n), BF16) for top, end in ranges], left, *weights, work=WORK)

        def transposed(x):
            step = min(512, x.shape[1])
            wide = t // 3 if t % 384 == 0 else t

            def kernel(x_ref, out_ref):
                for top in range(0, t, wide):
                    for lo in range(0, x.shape[1], step):
                        out_ref[lo : lo + step, top : top + wide] = x_ref[top : top + wide, lo : lo + step].T

            return call("transposed_train", kernel, [((x.shape[1], t), BF16)], x, work=WORK)[0]

        def scores(name, left, cols):
            def kernel(left_ref, train_ref, out_ref):
                out_ref[...] = dot(left_ref[...], train_ref[:, cols]).astype(BF16)

            return call(name, kernel, [((left.shape[0], cols.stop - cols.start), BF16)], left, trained[0])[0]

        def last_scores(kept, given):
            step = t // 3

            def kernel(kept_ref, given_ref, train_ref, out_ref):
                left = jnp.where(at(0), given_ref[...], kept_ref[...])
                for lo in range(0, t, step):
                    cols = slice(lo, lo + step)
                    out_ref[:, cols] = dot(left, train_ref[:, cols])

            return call("last_scores", kernel, [((m, t), F32)], kept, given, trained[0])[0]

        owners = [1, *[d ^ 1 for d in range(2, n_proj)], 0]
        ranges = {d: [(0, m)] for d in owners}
        chunks = [(d, *r) for d in owners for r in ranges[d]]
        n_chunks = len(chunks)
        last = n_chunks - 1
        rows = {0: targets}
        here, total, parts, moving = {}, {}, {}, {}

        def same(name, x):
            return elementwise(name, lambda v: v, x)

        def fetch(i, value):
            rows[owners[i]] = across(value, owners[i])

        def begin(i):
            d = owners[i]
            first = chunks.index((d, *ranges[d][0]))
            here.update(enumerate(condition(f"condition_{i}", rows[d], ranges[d]), first))

        def valid(c):
            return 0 <= c < n_chunks

        back_at = 2 * hops + LAG + (hops > 1)

        def outward(h, step):
            return step - back_at if h == 0 else step - 2 * hops + h - LAG

        def start_hop(h, step):
            c, back = step - h, outward(h, step)
            if h == 0 and c == 0:
                moving[h, step] = [along(x, hop_swaps[h]) for x in here[c]]
                return
            if valid(c) and valid(back):
                value = elementwise(f"merge_{step}", lambda a, b: jnp.where(at(h), a, b), here[c], total[back])
            elif valid(c):
                value = same(f"pass_{step}", here[c])
            elif valid(back):
                value = same(f"back_{step}", total[back])
            else:
                return
            moving[h, step] = along(value, hop_swaps[h])

        def end_hop(h, step):
            c, back = step - h, outward(h, step)

            def absorb(a, b):
                return jnp.where(at(h + 1), plus(a, b), a)

            if h == 0 and c == 0:
                low = update("absorb_0a", absorb, here[c][0], moving[h, step][0])

                def kernel(low_ref, a_ref, b_ref, out_ref):
                    out_ref[:, halves[0]] = low_ref[...]
                    out_ref[:, halves[1]] = absorb(a_ref[...], b_ref[...])

                here[c] = call("absorb_0b", kernel, [((m, n), BF16)], low, here[c][1], moving[h, step][1], work=WORK)[0]
            elif valid(c):
                here[c] = update(f"absorb_{step}", absorb, here[c], moving[h, step])
            if valid(back) and not (h == 0 and back == last):
                total[back] = update(f"adopt_{back}", lambda a, b: jnp.where(at(h), b, a), total[back], moving[h, step])

        def end_middle(c, step):
            total[c] = update(f"total_{c}", plus, here[c], moving["middle", step])

        def gather(c):
            for i, (cols, got) in enumerate(zip(pieces(c), parts[c])):
                first = c == 0 and i == 0

                def kernel(*refs):
                    *in_refs, out_ref = refs
                    if first:
                        out_ref[...] = jnp.zeros_like(out_ref)
                    else:
                        out_ref[...] = in_refs[0][...]
                    out_ref[:, cols] += in_refs[-1][...].astype(F32)

                before = [] if first else [parts["sum"]]
                parts["sum"] = call(f"gather_{c}_{i}", kernel, [((m, t), F32)], *before, got)[0]

        def pieces(c):
            return [slice(0, t)]

        def finish(c):
            parts[c] = []
            for i, cols in enumerate(pieces(c)):
                parts[c].append(across(scores(f"scores_{c}_{i}", total[c], cols), chunks[c][0]))

        for i in range(min(3, n_proj - 1)):
            fetch(i, targets)
        weights = []
        here[0] = []
        for side in (0, 1):
            out, half_weights = read_condition(rows[1], side)
            here[0].append(out)
            weights.append(half_weights)
        start_hop(0, 0)
        begin(1)
        start_hop(0, 1)
        trained = []
        for step in range(1, n_chunks + back_at):
            for h in reversed(range(hops)):
                end_hop(h, step - 1)
            c = step - hops
            if valid(c):
                moving["middle", step] = along(here[c], middle_swaps)
            for h in range(1, hops):
                start_hop(h, step)
            if step == 1:
                begin(n_proj - 1)
            if step + 1 < n_proj - 1:
                if step + 2 < n_proj - 1:
                    fetch(step + 2, same(f"own_rows_{step}", targets))
                begin(step + 1)
            c = step - 1 - back_at
            if valid(c):
                finish(c)
            if step == 2:
                trained.append(transposed(train))
            c = step - 1 - hops
            if valid(c):
                end_middle(c, step - 1)
            start_hop(0, step + 1)
        for c in range(last - 1):
            gather(c)
        value = last_scores(total[last], moving[0, last + back_at])
        gather(last - 1)

        def close(sum_ref, value_ref, out_ref):
            out_ref[...] = sum_ref[...] + value_ref[...]

        return call("close", close, [((m, t), F32)], parts["sum"], value)[0]

    return body


def solution(mesh):
    return jax.shard_map(
        make_body(mesh.shape["rows"], mesh.shape["proj"]),
        mesh=mesh,
        in_specs=(P("proj", "rows"), P(("groups", "rows"), "proj"), P(("groups", "rows"), "proj")),
        out_specs=P("proj", ("groups", "rows")),
        check_vma=False,
    )
```
